128 devices in a mesh: range: 32 (over z, x, core), cross: 4 (over y).
Axes of the slice: x: 4, y: 4, z: 4, core: 2. Of those that a mesh axis runs over, the one named last changes fastest.
Arguments:
- surface_field: bfloat16 [131072, 1024], P(('range', 'cross')), may hold values from -6 to 6
- point_count: int32 [128], P(('range', 'cross')), may hold values from 512 to 1024, as said below
- far_rank: int32 [128, 128], P(('range', 'cross')), may hold values from 4 to 16, as said below
- source_factor: bfloat16 [2, 2048, 131072], P(None, None, ('range', 'cross')), may hold values from -0.1875 to 0.1875
- target_factor: bfloat16 [2, 131072, 2048], P(None, ('range', 'cross')), may hold values from -0.5 to 0.5
- near_blocks: bfloat16 [2, 131072, 3, 128], P(None, ('range', 'cross')), may hold values from -0.3125 to 0.3125
- near_index: int32 [1024, 3], P(('range', 'cross')), may hold values from 0 to 11
Outputs:
- scattered: bfloat16 [131072, 1024], P(('range', 'cross'))
The draws below stay inside these ranges and needn't reach their ends.
Inputs may be any that keep to these rules, and one draw needn't show every extreme that they name: `point_count`: each count lies between half a box and a full box; some box is full. `far_rank`: every source box has a pair of full rank 16.
All inputs are finite; a program needn't handle non-finite values.
Results may differ from the reference program's by a relative error of at most 0.0043.
Values may be sent and summed in bfloat16 or wider, within the bound.
No kernel may reach another device: no remote copies, remote signals or barrier semaphores. Data moves between devices by JAX's collectives and lax.ppermute only.
A program may use at most 128 MiB of HBM per device.

```python
import jax
import jax.numpy as jnp
from jax import lax

P_DEV = 1024
RANK = 16
NEAR_B = 128
NB = 3
HALO_BLK = 2
BOXES = 128
POINTS = 131072
BLK = 8
COLS = 1024
N_RANGE = 32
N_CROSS = 4


def draw_point_count(key, part):
    key = jax.random.fold_in(key, 11)
    boxes = N_RANGE * N_CROSS
    counts = jax.random.randint(jax.random.fold_in(key, 1), (boxes,), P_DEV // 2, P_DEV + 1)
    full_box = jax.random.randint(jax.random.fold_in(key, 2), (), 0, boxes)
    return counts.at[full_box].set(P_DEV).astype(jnp.int32)


def draw_far_rank(key, part):
    key = jax.random.fold_in(key, 23)
    boxes = N_RANGE * N_CROSS
    lowest = max(RANK // 4, 1)
    ranks = jax.random.randint(jax.random.fold_in(key, 1), (boxes, boxes), lowest, RANK + 1)
    column = jax.random.randint(jax.random.fold_in(key, 2), (boxes, 1), 0, boxes)
    places = jnp.arange(boxes, dtype=jnp.int32)[None, :]
    return jnp.where(places == column, RANK, ranks).astype(jnp.int32)


def plant(values, stream_key, smallest, high):
    longest = values.shape.index(max(values.shape))
    spots = []
    for shift in (0, 1):
        where = [jax.random.randint(jax.random.fold_in(stream_key, axis), (), 0, length) for axis, length in enumerate(values.shape)]
        where[longest] = (where[longest] + shift) % values.shape[longest]
        spots.append(tuple(where))
    return values.at[spots[0]].set(smallest).at[spots[1]].set(high)


def spiked(values, rng, source, target, blocks, factor):
    owner, partner = [(jnp.arange(values.shape[position]) // (values.shape[position] // blocks)).reshape([-1 if axis == position else 1 for axis in range(values.ndim)]) for position in (source, target)]
    chosen = jax.random.permutation(rng, blocks)[partner]
    strong = (owner == chosen) | (owner == (partner + blocks // 2) % blocks)
    return jnp.where(strong, factor * values, values)


def block_levels(own_key, shape, split, smallest, largest):
    def one(dim, shards_of):
        steps = jax.random.uniform(jax.random.fold_in(jax.random.fold_in(own_key, 6), dim), (shards_of,), jnp.float32, smallest / len(split), largest / len(split))
        return jnp.repeat(jnp.exp(steps), shape[dim] // shards_of).reshape((-1,) + (1,) * (len(shape) - dim - 1))

    level = one(*split[0])
    for cut in split[1:]:
        level = level * one(*cut)
    return level


def noise(rng, dims, scale, limit, cuts=(), kind=jnp.bfloat16):
    loudness = block_levels(rng, dims, cuts, -0.22, 0.18) if cuts else 1.0
    drawn = jax.random.normal(rng, dims, jnp.float32) * scale * loudness
    return jnp.minimum(jnp.maximum(drawn, -limit), limit).astype(kind)


def gaussian_with(stream_key, shape, deviation, bound, cuts, heavy, kind=jnp.bfloat16):
    array = deviation * jax.random.normal(stream_key, shape, jnp.float32)
    if cuts:
        array = array * block_levels(stream_key, shape, cuts, -0.22, 0.18)
    return jnp.clip(spiked(array, jax.random.fold_in(stream_key, 3), *heavy), -bound, bound).astype(kind)


def setup_inputs(seed: int = 0) -> dict:
    key_of = jax.random.split(jax.random.key(seed), 8)
    surface_field = noise(key_of[0], (POINTS, COLS), 1.0, 6.0, ((0, 128),))
    point_count = draw_point_count(jax.random.fold_in(key_of[7], 71), 0)
    far_rank = draw_far_rank(jax.random.fold_in(key_of[7], 71), 0)
    source_factor = noise(key_of[3], (2, BOXES * RANK, POINTS), P_DEV ** -0.5, 0.1875, ((2, 128),))
    target_factor = gaussian_with(key_of[4], (2, POINTS, BOXES * RANK), (BOXES * RANK) ** -0.5, 0.5, ((1, 128),), (2, 1, 128, 5.5))
    near_blocks = noise(key_of[5], (2, POINTS, NB, NEAR_B), (NB * NEAR_B) ** -0.5, 0.3125, ((1, 128),))
    near_index = plant(jax.random.randint(key_of[6], (BOXES * BLK, NB), 0, BLK + 2 * HALO_BLK), jax.random.fold_in(key_of[6], 1), 0, (BLK + 2 * HALO_BLK) - 1).astype(jnp.int32)
    return {"surface_field": surface_field, "point_count": point_count, "far_rank": far_rank, "source_factor": source_factor, "target_factor": target_factor, "near_blocks": near_blocks, "near_index": near_index}


def rotate(block):
    half = block.shape[-1] // 2
    return jnp.concatenate([-block[..., half:], block[..., :half]], axis=-1)


def reference(surface_field, point_count, far_rank, source_factor, target_factor, near_blocks, near_index):
    boxes = N_RANGE * N_CROSS
    slots = jnp.arange(P_DEV, dtype=jnp.int32)
    live = (slots[None, :] < point_count[:, None]).reshape(boxes * P_DEV, 1)
    field = surface_field * live.astype(jnp.bfloat16)
    rank_keep = jnp.arange(RANK, dtype=jnp.int32)[None, None, :] < far_rank[:, :, None]

    def source_box(box):
        start = (box * P_DEV).astype(jnp.int32)
        part = lax.dynamic_slice_in_dim(field, start, P_DEV, 0)
        factor = lax.dynamic_slice_in_dim(source_factor, start, P_DEV, 2)
        coeffs = jnp.dot(factor[0], part, preferred_element_type=jnp.float32)
        coeffs = coeffs + jnp.dot(factor[1], rotate(part), preferred_element_type=jnp.float32)
        keep = rank_keep[box].reshape(boxes * RANK, 1)
        return jnp.where(keep, coeffs, jnp.float32(0.0)).astype(jnp.bfloat16).reshape(boxes, RANK, COLS)

    coeffs = lax.map(source_box, jnp.arange(boxes, dtype=jnp.int32))

    def target_box(box):
        arrived = coeffs[:, box].reshape(boxes * RANK, COLS)
        factor = lax.dynamic_slice_in_dim(target_factor, (box * P_DEV).astype(jnp.int32), P_DEV, 1)
        result = jnp.dot(factor[0], arrived, preferred_element_type=jnp.float32)
        return result + jnp.dot(factor[1], rotate(arrived), preferred_element_type=jnp.float32)

    far = lax.map(target_box, jnp.arange(boxes, dtype=jnp.int32)).reshape(boxes * P_DEV, COLS)

    tiles = field.reshape(N_RANGE, N_CROSS, P_DEV, COLS)
    width = HALO_BLK * NEAR_B
    zero_rim = jnp.zeros((N_RANGE, 1, width, COLS), jnp.bfloat16)
    before = jnp.concatenate([zero_rim, tiles[:, :-1, P_DEV - width:]], axis=1)
    after = jnp.concatenate([tiles[:, 1:, :width], zero_rim], axis=1)
    window = jnp.concatenate([before, tiles, after], axis=2).reshape(boxes, BLK + 2 * HALO_BLK, NEAR_B, COLS)
    index = near_index.reshape(boxes, BLK, NB)
    blocks = near_blocks.reshape(2, boxes, BLK, NEAR_B, NB, NEAR_B)

    def near_box(box):
        picked = window[box][index[box]].astype(jnp.float32)
        mats = blocks[:, box].astype(jnp.float32)
        result = jnp.einsum('bink,bnkc->bic', mats[0], picked)
        result = result + jnp.einsum('bink,bnkc->bic', mats[1], rotate(picked))
        return result.reshape(P_DEV, COLS)

    near = lax.map(near_box, jnp.arange(boxes, dtype=jnp.int32)).reshape(boxes * P_DEV, COLS)
    return ((near + far) * live.astype(jnp.float32)).astype(jnp.bfloat16)
```

```python
import functools

import jax
import jax.numpy as jnp
from jax import lax
from jax.experimental import pallas as pl
from jax.experimental.pallas import tpu as pltpu
from jax.sharding import PartitionSpec as P

RANK = 16
NEAR_B = 128
NB = 3
HALO_BLK = 2
AXES = ("range", "cross")
MIB = 1024 * 1024


def params(mib):
    return pltpu.CompilerParams(vmem_limit_bytes=mib * MIB)


def cost(flops, bytes_accessed):
    return pl.CostEstimate(flops=flops, bytes_accessed=bytes_accessed, transcendentals=0)


def dot(a, b):
    return jnp.dot(a, b, preferred_element_type=jnp.float32)


def coeffs_kernel(rows, depth, count_ref, rank_ref, x_hbm, s_hbm, out_hbm, x_buf, s_buf, held, x_sem, s_sem, out_sem):
    points, cols = x_buf.shape
    half = cols // 2
    tiles = s_buf.shape[1] // rows
    groups = rows // RANK

    def get_x(k):
        place = pl.ds(k * depth, depth)
        return pltpu.make_async_copy(x_hbm.at[place], x_buf.at[place], x_sem.at[k])

    def get_s(tile):
        place = pl.ds(pl.multiple_of(tile * rows, rows), rows)
        return pltpu.make_async_copy(s_hbm.at[:, place], s_buf.at[:, place], s_sem.at[tile])

    def put(tile, slot):
        place = pl.ds(pl.multiple_of(tile * rows, rows), rows)
        return pltpu.make_async_copy(held.at[slot], out_hbm.at[place], out_sem.at[slot])

    def finish(tile, slot, pq):
        place = lax.broadcasted_iota(jnp.int32, (RANK, half), 0)
        for group in range(groups):
            keep = place < rank_ref[tile * groups + group]
            p = pq[group * RANK : (group + 1) * RANK]
            q = pq[rows + group * RANK : rows + (group + 1) * RANK]
            own = slice(group * RANK, (group + 1) * RANK)
            held[slot, own, :half] = jnp.where(keep, p[:, :half] - q[:, half:], 0.0).astype(jnp.bfloat16)
            held[slot, own, half:] = jnp.where(keep, p[:, half:] + q[:, :half], 0.0).astype(jnp.bfloat16)
        put(tile, slot).start()

    parts = points // depth
    get_x(0).start()
    get_s(0).start()
    for k in range(1, parts):
        get_x(k).start()
    for tile in range(1, tiles):
        get_s(tile).start()
    pq = jnp.zeros((2 * rows, cols), jnp.float32)
    get_s_done = False
    for k in range(parts):
        get_x(k).wait()
        own = slice(k * depth, (k + 1) * depth)
        live = lax.broadcasted_iota(jnp.int32, (depth, cols), 0) + k * depth < count_ref[0]
        x = jnp.where(live, x_buf[own].astype(jnp.float32), 0.0).astype(jnp.bfloat16)
        x_buf[own] = x
        if not get_s_done:
            get_s(0).wait()
            get_s_done = True
        pq += dot(s_buf[:, :rows, own].reshape(2 * rows, depth), x)
    finish(0, 0, pq)

    def body(tile, carry):
        slot = lax.rem(tile, 2)
        get_s(tile).wait()
        place = pl.ds(pl.multiple_of(tile * rows, rows), rows)
        full = dot(s_buf[:, place].reshape(2 * rows, points), x_buf[...])

        @pl.when(tile >= 2)
        def _():
            put(tile - 2, slot).wait()

        finish(tile, slot, full)
        return carry

    lax.fori_loop(1, tiles, body, 0)
    for tile in (tiles - 2, tiles - 1):
        put(tile, tile % 2).wait()


def coefficients(count, rank, field, factor, rows=256, depth=256):
    points, cols = field.shape
    total = factor.shape[1]
    return pl.pallas_call(
        functools.partial(coeffs_kernel, rows, depth),
        out_shape=jax.ShapeDtypeStruct((total, cols), jnp.bfloat16),
        in_specs=[pl.BlockSpec(memory_space=pltpu.SMEM)] * 2 + [pl.BlockSpec(memory_space=pl.ANY)] * 2,
        out_specs=pl.BlockSpec(memory_space=pl.ANY),
        scratch_shapes=[
            pltpu.VMEM((points, cols), jnp.bfloat16),
            pltpu.VMEM((2, total, points), jnp.bfloat16),
            pltpu.VMEM((2, rows, cols), jnp.bfloat16),
            pltpu.SemaphoreType.DMA((points // depth,)),
            pltpu.SemaphoreType.DMA((total // rows,)),
            pltpu.SemaphoreType.DMA((2,)),
        ],
        compiler_params=params(60),
        cost_estimate=cost(4 * total * points * cols, 4 * total * points + 2 * (points + total) * cols),
        name="coeffs",
    )(count, rank, field, factor)


def near_kernel(index_ref, count_ref, low_ref, x_ref, high_ref, n_ref, out_ref, window):
    block = pl.program_id(0)
    points, cols = x_ref.shape
    half = cols // 2
    rim = HALO_BLK

    @pl.when(block == 0)
    def _():
        window[:rim] = low_ref[...].reshape(rim, NEAR_B, cols)
        window[rim + points // NEAR_B :] = high_ref[...].reshape(rim, NEAR_B, cols)
        for b in range(points // NEAR_B):
            live = lax.broadcasted_iota(jnp.int32, (NEAR_B, cols), 0) + b * NEAR_B < count_ref[0]
            part = x_ref[b * NEAR_B : (b + 1) * NEAR_B].astype(jnp.float32)
            window[rim + b] = jnp.where(live, part, 0.0).astype(jnp.bfloat16)

    p = jnp.zeros((NEAR_B, cols), jnp.float32)
    q = jnp.zeros((NEAR_B, cols), jnp.float32)
    for k in range(NB):
        x = window[index_ref[block * NB + k]]
        p += dot(n_ref[0, k], x)
        q += dot(n_ref[1, k], x)
    out_ref[:, :half] = p[:, :half] - q[:, half:]
    out_ref[:, half:] = p[:, half:] + q[:, :half]


def near_field(index, count, low, field, high, blocks):
    points, cols = field.shape
    rim = HALO_BLK * NEAR_B
    return pl.pallas_call(
        near_kernel,
        out_shape=jax.ShapeDtypeStruct((points, cols), jnp.float32),
        grid_spec=pltpu.PrefetchScalarGridSpec(
            num_scalar_prefetch=2,
            grid=(points // NEAR_B,),
            in_specs=[
                pl.BlockSpec((rim, cols), lambda i, *_: (0, 0)),
                pl.BlockSpec((points, cols), lambda i, *_: (0, 0)),
                pl.BlockSpec((rim, cols), lambda i, *_: (0, 0)),
                pl.BlockSpec((2, NB, NEAR_B, NEAR_B), lambda i, *_: (0, 0, i, 0)),
            ],
            out_specs=pl.BlockSpec((NEAR_B, cols), lambda i, *_: (i, 0)),
            scratch_shapes=[pltpu.VMEM((points // NEAR_B + 2 * HALO_BLK, NEAR_B, cols), jnp.bfloat16)],
        ),
        compiler_params=params(24),
        cost_estimate=cost(60_000_000_000, 6 * points * cols + 4 * points * NB * NEAR_B),
        name="near",
    )(index, count, low, field, high, blocks)


def far_kernel(rows, part, count_ref, c_hbm, t_hbm, n_hbm, out_hbm, c_buf, t_buf, n_buf, held, c_sem, f_sem, t_sem, n_sem, out_sem):
    depth, cols = c_buf.shape
    points = t_buf.shape[1]
    half = cols // 2
    tiles = points // rows
    parts = depth // part

    def get_c(k):
        place = pl.ds(k * part, part)
        return pltpu.make_async_copy(c_hbm.at[place], c_buf.at[place], c_sem.at[k])

    def get_first(k):
        place = pl.ds(k * part, part)
        return pltpu.make_async_copy(t_hbm.at[:, pl.ds(0, rows), place], t_buf.at[:, pl.ds(0, rows), place], f_sem.at[k])

    def get_t(tile):
        place = pl.ds(tile * rows, rows)
        return pltpu.make_async_copy(t_hbm.at[:, place], t_buf.at[:, place], t_sem.at[tile])

    def get_n(tile):
        place = pl.ds(tile * rows, rows)
        return pltpu.make_async_copy(n_hbm.at[place], n_buf.at[place], n_sem.at[tile])

    def put(tile):
        place = pl.ds(tile * rows, rows)
        return pltpu.make_async_copy(held.at[tile % 2], out_hbm.at[place], out_sem.at[tile % 2])

    def finish(tile, pq):
        get_n(tile).wait()
        if tile >= 2:
            put(tile - 2).wait()
        own = slice(tile * rows, (tile + 1) * rows)
        live = lax.broadcasted_iota(jnp.int32, (rows, half), 0) + tile * rows < count_ref[0]
        real = pq[:rows, :half] - pq[rows:, half:] + n_buf[own, :half]
        imag = pq[:rows, half:] + pq[rows:, :half] + n_buf[own, half:]
        held[tile % 2, :, :half] = jnp.where(live, real, 0.0).astype(jnp.bfloat16)
        held[tile % 2, :, half:] = jnp.where(live, imag, 0.0).astype(jnp.bfloat16)
        put(tile).start()

    for k in range(parts):
        get_c(k).start()
        get_first(k).start()
    get_n(0).start()
    for tile in range(1, tiles):
        get_t(tile).start()
        get_n(tile).start()
    pq = jnp.zeros((2 * rows, cols), jnp.float32)
    for k in range(parts):
        get_c(k).wait()
        get_first(k).wait()
        own = slice(k * part, (k + 1) * part)
        pq += dot(t_buf[:, :rows, own].reshape(2 * rows, part), c_buf[own])
    finish(0, pq)
    for tile in range(1, tiles):
        get_t(tile).wait()
        finish(tile, dot(t_buf[:, tile * rows : (tile + 1) * rows].reshape(2 * rows, depth), c_buf[...]))
    for tile in range(tiles - 2, tiles):
        put(tile).wait()


def far_field(count, arrived, factor, near, rows=256, part=512):
    points, cols = near.shape
    depth = arrived.shape[0]
    return pl.pallas_call(
        functools.partial(far_kernel, rows, part),
        out_shape=jax.ShapeDtypeStruct((points, cols), jnp.bfloat16),
        in_specs=[pl.BlockSpec(memory_space=pltpu.SMEM)] + [pl.BlockSpec(memory_space=pl.ANY)] * 3,
        out_specs=pl.BlockSpec(memory_space=pl.ANY),
        scratch_shapes=[
            pltpu.VMEM((depth, cols), jnp.bfloat16),
            pltpu.VMEM((2, points, depth), jnp.bfloat16),
            pltpu.VMEM((points, cols), jnp.float32),
            pltpu.VMEM((2, rows, cols), jnp.bfloat16),
            pltpu.SemaphoreType.DMA((depth // part,)),
            pltpu.SemaphoreType.DMA((depth // part,)),
            pltpu.SemaphoreType.DMA((points // rows,)),
            pltpu.SemaphoreType.DMA((points // rows,)),
            pltpu.SemaphoreType.DMA((2,)),
        ],
        compiler_params=params(60),
        cost_estimate=cost(4 * points * depth * cols, 4 * points * depth + 2 * depth * cols + 6 * points * cols),
        name="far",
    )(count, arrived, factor, near)


def halo(field, count):
    points = field.shape[0]
    rim = HALO_BLK * NEAR_B
    devices = lax.axis_size("cross")
    forward = [(i, i + 1) for i in range(devices - 1)]
    backward = [(target, source) for source, target in forward]
    rows = lax.broadcasted_iota(jnp.int32, (rim, 1), 0)
    zero = jnp.zeros((), jnp.bfloat16)
    last = jnp.where(rows + (points - rim) < count[0], field[points - rim :], zero)
    return lax.ppermute(last, "cross", forward), lax.ppermute(field[:rim], "cross", backward)


def shards(surface_field, point_count, far_rank, source_factor, target_factor, near_blocks, near_index):
    boxes = far_rank.shape[1]
    cols = surface_field.shape[1]
    low, high = halo(surface_field, point_count)
    coeffs = coefficients(point_count, far_rank.reshape(boxes), surface_field, source_factor)
    coeffs = coeffs.reshape(boxes, RANK, cols)
    arrived = lax.all_to_all(coeffs, AXES, split_axis=0, concat_axis=0, tiled=True)
    near = near_field(
        near_index.reshape(-1), point_count, low, surface_field, high, jnp.transpose(near_blocks, (0, 2, 1, 3))
    )
    return far_field(point_count, arrived.reshape(boxes * RANK, cols), target_factor, near)


def solution(mesh):
    return jax.shard_map(
        shards,
        mesh=mesh,
        in_specs=(
            P(AXES, None),
            P(AXES),
            P(AXES, None),
            P(None, None, AXES),
            P(None, AXES, None),
            P(None, AXES, None, None),
            P(AXES, None),
        ),
        out_specs=P(AXES, None),
        check_vma=False,
    )
```

```python
import functools

import jax
import jax.numpy as jnp
from jax import lax
from jax.experimental import pallas as pl
from jax.experimental.pallas import tpu as pltpu
from jax.sharding import PartitionSpec as P

RANK = 16
NEAR_B = 128
NB = 3
HALO_BLK = 2
AXES = ("range", "cross")
MIB = 1024 * 1024


def params(mib):
    return pltpu.CompilerParams(vmem_limit_bytes=mib * MIB)


def cost(flops, bytes_accessed):
    return pl.CostEstimate(flops=flops, bytes_accessed=bytes_accessed, transcendentals=0)


def dot(a, b):
    return jnp.dot(a, b, preferred_element_type=jnp.float32)


def coeffs_kernel(
    tiles, depth, count_ref, rank_ref, x_hbm, s_hbm, out_hbm, low_hbm, high_hbm,
    x_buf, s_buf, held, x_sem, s_sem, out_sem, edge_sem
):
    points, cols = x_hbm.shape
    width = cols // 2
    parts = points // depth
    rim = low_hbm.shape[0]
    first = 0
    edges = (
        pltpu.make_async_copy(x_buf.at[pl.ds(0, rim)], low_hbm, edge_sem.at[0]),
        pltpu.make_async_copy(x_buf.at[pl.ds(points - rim, rim)], high_hbm, edge_sem.at[1]),
    )

    def rows_of(tile):
        return sum(tiles[:tile]), tiles[tile]

    def get_x(k, side):
        place = pl.ds(k * depth, depth)
        there = pl.ds(first + side * (cols // 2), width)
        return pltpu.make_async_copy(
            x_hbm.at[place, there], x_buf.at[place, pl.ds(side * width, width)], x_sem.at[k, side]
        )

    def get_s(tile):
        place = pl.ds(*rows_of(tile))
        return pltpu.make_async_copy(s_hbm.at[:, place], s_buf.at[:, place], s_sem.at[tile])

    def put(tile):
        place = pl.ds(*rows_of(tile))
        return pltpu.make_async_copy(held.at[place], out_hbm.at[place], out_sem.at[tile])

    def finish(tile, total):
        start, rows = rows_of(tile)
        place = lax.broadcasted_iota(jnp.int32, (RANK, 2 * width), 0)
        for group in range(rows // RANK):
            keep = place < rank_ref[start // RANK + group]
            part = total[group * RANK : (group + 1) * RANK]
            held[start + group * RANK : start + (group + 1) * RANK] = jnp.where(keep, part, 0.0).astype(jnp.bfloat16)
        put(tile).start()

    for k in range(min(parts, 2)):
        get_x(k, 0).start()
        get_x(k, 1).start()
        if k == 0:
            get_s(0).start()
    total = jnp.zeros((tiles[0], 2 * width), jnp.float32)
    for k in range(parts):
        get_x(k, 0).wait()
        get_x(k, 1).wait()
        own = slice(k * depth, (k + 1) * depth)
        turned = slice(points + k * depth, points + (k + 1) * depth)
        x = x_buf[own]
        if 2 * k * depth >= points:
            live = lax.broadcasted_iota(jnp.int32, x.shape, 0) + k * depth < count_ref[0]
            x = jnp.where(live, x.astype(jnp.float32), 0.0).astype(jnp.bfloat16)
            x_buf[own] = x
        x_buf[turned, :width] = -x[:, width:]
        x_buf[turned, width:] = x[:, :width]
        if k == 0:
            get_s(0).wait()
        if k + 2 < parts:
            get_x(k + 2, 0).start()
            get_x(k + 2, 1).start()
        if k == parts - 2:
            get_s(1).start()
        total += dot(s_buf[0, : tiles[0], own], x_buf[own]) + dot(s_buf[1, : tiles[0], own], x_buf[turned])
    finish(0, total)
    for edge in edges:
        edge.start()
    for tile in range(1, len(tiles)):
        start, rows = rows_of(tile)
        get_s(tile).wait()
        if tile + 1 < len(tiles):
            get_s(tile + 1).start()
        own = slice(start, start + rows)
        finish(tile, dot(jnp.concatenate([s_buf[0, own], s_buf[1, own]], axis=1), x_buf[...]))
    for edge in edges:
        edge.wait()
    for tile in range(len(tiles)):
        put(tile).wait()


def coefficients(count, rank, field, factor, depth=512, tiles=(256, 512, 1024, 256)):
    points, cols = field.shape
    total = factor.shape[1]
    width = cols // 2
    edge = jax.ShapeDtypeStruct((HALO_BLK * NEAR_B, cols), jnp.bfloat16)
    return pl.pallas_call(
        functools.partial(coeffs_kernel, tiles, depth),
        out_shape=[jax.ShapeDtypeStruct((total, cols), jnp.bfloat16), edge, edge],
        in_specs=[pl.BlockSpec(memory_space=pltpu.SMEM)] * 2 + [pl.BlockSpec(memory_space=pl.ANY)] * 2,
        out_specs=[pl.BlockSpec(memory_space=pl.ANY)] * 3,
        scratch_shapes=[
            pltpu.VMEM((2 * points, 2 * width), jnp.bfloat16),
            pltpu.VMEM((2, total, points), jnp.bfloat16),
            pltpu.VMEM((total, 2 * width), jnp.bfloat16),
            pltpu.SemaphoreType.DMA((points // depth, 2)),
            pltpu.SemaphoreType.DMA((len(tiles),)),
            pltpu.SemaphoreType.DMA((len(tiles),)),
            pltpu.SemaphoreType.DMA((2,)),
        ],
        compiler_params=params(60),
        cost_estimate=cost(8 * total * points * width, 4 * total * points + 4 * (points + total) * width),
        name="coeffs",
    )(count, rank, field, factor)


def near_kernel(index_ref, count_ref, low_ref, x_ref, high_ref, n_ref, out_ref, window):
    block = pl.program_id(0)
    points, cols = x_ref.shape
    half = cols // 2
    rim = HALO_BLK

    @pl.when(block == 0)
    def _():
        window[:rim] = low_ref[...].reshape(rim, NEAR_B, cols)
        window[rim + points // NEAR_B :] = high_ref[...].reshape(rim, NEAR_B, cols)
        for b in range(points // NEAR_B):
            live = lax.broadcasted_iota(jnp.int32, (NEAR_B, cols), 0) + b * NEAR_B < count_ref[0]
            part = x_ref[b * NEAR_B : (b + 1) * NEAR_B].astype(jnp.float32)
            window[rim + b] = jnp.where(live, part, 0.0).astype(jnp.bfloat16)

    p = jnp.zeros((NEAR_B, cols), jnp.float32)
    q = jnp.zeros((NEAR_B, cols), jnp.float32)
    for k in range(NB):
        x = window[index_ref[block * NB + k]]
        p += dot(n_ref[0, k], x)
        q += dot(n_ref[1, k], x)
    out_ref[:, :half] = p[:, :half] - q[:, half:]
    out_ref[:, half:] = p[:, half:] + q[:, :half]


def near_field(index, count, low, field, high, blocks):
    points, cols = field.shape
    rim = HALO_BLK * NEAR_B
    return pl.pallas_call(
        near_kernel,
        out_shape=jax.ShapeDtypeStruct((points, cols), jnp.float32),
        grid_spec=pltpu.PrefetchScalarGridSpec(
            num_scalar_prefetch=2,
            grid=(points // NEAR_B,),
            in_specs=[
                pl.BlockSpec((rim, cols), lambda i, *_: (0, 0)),
                pl.BlockSpec((points, cols), lambda i, *_: (0, 0)),
                pl.BlockSpec((rim, cols), lambda i, *_: (0, 0)),
                pl.BlockSpec((2, NB, NEAR_B, NEAR_B), lambda i, *_: (0, 0, i, 0)),
            ],
            out_specs=pl.BlockSpec((NEAR_B, cols), lambda i, *_: (i, 0)),
            scratch_shapes=[pltpu.VMEM((points // NEAR_B + 2 * HALO_BLK, NEAR_B, cols), jnp.bfloat16)],
        ),
        compiler_params=params(24),
        cost_estimate=cost(60_000_000_000, 6 * points * cols + 4 * points * NB * NEAR_B),
        name="near",
    )(index, count, low, field, high, blocks)


def far_kernel(first, tiles, part, count_ref, c_hbm, t_hbm, n_hbm, *refs):
    out_hbm, c_buf, t_buf, n_buf, held, c_sem, f_sem, t_sem, n_sem, out_sem = refs[-10:]
    depth = c_hbm.shape[0]
    cols = n_hbm.shape[1]
    width = c_hbm.shape[1] // 2
    parts = depth // part

    def rows_of(tile):
        return sum(tiles[:tile]), tiles[tile]

    def get_c(k):
        place = pl.ds(k * part, part)
        return pltpu.make_async_copy(c_hbm.at[place], c_buf.at[place], c_sem.at[k])

    def get_first(k):
        rows, place = pl.ds(0, tiles[0]), pl.ds(k * part, part)
        return pltpu.make_async_copy(t_hbm.at[:, rows, place], t_buf.at[:, rows, place], f_sem.at[k])

    def get_t(tile):
        place = pl.ds(*rows_of(tile))
        return pltpu.make_async_copy(t_hbm.at[:, place], t_buf.at[:, place], t_sem.at[tile])

    def get_n(tile, side):
        place = pl.ds(*rows_of(tile))
        there, here = pl.ds(first + side * (cols // 2), width), pl.ds(side * width, width)
        return pltpu.make_async_copy(n_hbm.at[place, there], n_buf.at[place, here], n_sem.at[tile, side])

    def put(tile, side):
        place = pl.ds(*rows_of(tile))
        there, here = pl.ds(first + side * (cols // 2), width), pl.ds(side * width, width)
        return pltpu.make_async_copy(held.at[place, here], out_hbm.at[place, there], out_sem.at[tile, side])

    def finish(tile, pq):
        start, rows = rows_of(tile)
        get_n(tile, 0).wait()
        get_n(tile, 1).wait()
        own = slice(start, start + rows)
        live = lax.broadcasted_iota(jnp.int32, (rows, width), 0) + start < count_ref[0]
        real = pq[:rows, :width] - pq[rows:, width:] + n_buf[own, :width]
        imag = pq[:rows, width:] + pq[rows:, :width] + n_buf[own, width:]
        held[own, :width] = jnp.where(live, real, 0.0).astype(jnp.bfloat16)
        held[own, width:] = jnp.where(live, imag, 0.0).astype(jnp.bfloat16)
        put(tile, 0).start()
        put(tile, 1).start()

    def get_more(tile):
        get_t(tile).start()
        get_n(tile, 0).start()
        get_n(tile, 1).start()

    for k in range(min(parts, 2)):
        get_c(k).start()
        get_first(k).start()
    pq = jnp.zeros((2 * tiles[0], 2 * width), jnp.float32)
    for k in range(parts):
        get_c(k).wait()
        get_first(k).wait()
        if k + 2 < parts:
            get_c(k + 2).start()
            get_first(k + 2).start()
        if k == parts - 2:
            get_n(0, 0).start()
            get_n(0, 1).start()
            get_more(1)
        own = slice(k * part, (k + 1) * part)
        pq += dot(t_buf[:, : tiles[0], own].reshape(2 * tiles[0], part), c_buf[own])
    finish(0, pq)
    for tile in range(1, len(tiles)):
        start, rows = rows_of(tile)
        get_t(tile).wait()
        if tile + 1 < len(tiles):
            get_more(tile + 1)
        finish(tile, dot(t_buf[:, start : start + rows].reshape(2 * rows, depth), c_buf[...]))
    for tile in range(len(tiles)):
        put(tile, 0).wait()
        put(tile, 1).wait()


def far_field(first, count, arrived, factor, near, out, part=512, tiles=(256, 512, 256)):
    points, cols = near.shape
    depth, wide = arrived.shape
    kept = [] if out is None else [out]
    return pl.pallas_call(
        functools.partial(far_kernel, first, tiles, part),
        out_shape=jax.ShapeDtypeStruct((points, cols), jnp.bfloat16),
        in_specs=[pl.BlockSpec(memory_space=pltpu.SMEM)] + [pl.BlockSpec(memory_space=pl.ANY)] * (3 + len(kept)),
        out_specs=pl.BlockSpec(memory_space=pl.ANY),
        scratch_shapes=[
            pltpu.VMEM((depth, wide), jnp.bfloat16),
            pltpu.VMEM((2, points, depth), jnp.bfloat16),
            pltpu.VMEM((points, wide), jnp.float32),
            pltpu.VMEM((points, wide), jnp.bfloat16),
            pltpu.SemaphoreType.DMA((depth // part,)),
            pltpu.SemaphoreType.DMA((depth // part,)),
            pltpu.SemaphoreType.DMA((len(tiles),)),
            pltpu.SemaphoreType.DMA((len(tiles), 2)),
            pltpu.SemaphoreType.DMA((len(tiles), 2)),
        ],
        input_output_aliases={4: 0} if kept else {},
        compiler_params=params(60),
        cost_estimate=cost(4 * points * depth * wide, 4 * points * depth + 2 * depth * wide + 6 * points * wide),
        name=f"far_{first}",
    )(count, arrived, factor, near, *kept)


def halo(first, last):
    devices = lax.axis_size("cross")
    forward = [(i, i + 1) for i in range(devices - 1)]
    backward = [(target, source) for source, target in forward]
    return lax.ppermute(last, "cross", forward), lax.ppermute(first, "cross", backward)


def shards(surface_field, point_count, far_rank, source_factor, target_factor, near_blocks, near_index):
    boxes = far_rank.shape[1]
    cols = surface_field.shape[1]
    coeffs, first, last = coefficients(point_count, far_rank.reshape(boxes), surface_field, source_factor)
    low, high = halo(first, last)
    arrived = lax.all_to_all(coeffs.reshape(boxes, RANK, cols), AXES, split_axis=0, concat_axis=0, tiled=True)
    near = near_field(
        near_index.reshape(-1), point_count, low, surface_field, high, jnp.transpose(near_blocks, (0, 2, 1, 3))
    )
    return far_field(0, point_count, arrived.reshape(boxes * RANK, cols), target_factor, near, None)


def solution(mesh):
    return jax.shard_map(
        shards,
        mesh=mesh,
        in_specs=(
            P(AXES, None),
            P(AXES),
            P(AXES, None),
            P(None, None, AXES),
            P(None, AXES, None),
            P(None, AXES, None, None),
            P(AXES, None),
        ),
        out_specs=P(AXES, None),
        check_vma=False,
    )
```

```python
import functools

import jax
import jax.numpy as jnp
from jax import lax
from jax.experimental import pallas as pl
from jax.experimental.pallas import tpu as pltpu
from jax.sharding import PartitionSpec as P

RANK = 16
NEAR_B = 128
NB = 3
HALO_BLK = 2
AXES = ("range", "cross")
MIB = 1024 * 1024


def params(mib):
    return pltpu.CompilerParams(vmem_limit_bytes=mib * MIB)


def cost(flops, bytes_accessed):
    return pl.CostEstimate(flops=flops, bytes_accessed=bytes_accessed, transcendentals=0)


def dot(a, b):
    return jnp.dot(a, b, preferred_element_type=jnp.float32)


def coeffs_kernel(
    tiles, depth, count_ref, rank_ref, x_hbm, s_hbm, out_hbm, low_hbm, high_hbm,
    x_buf, s_buf, held, x_sem, s_sem, out_sem, edge_sem
):
    points, cols = x_hbm.shape
    width = cols // 2
    parts = points // depth
    rim = low_hbm.shape[0]
    first = 0
    edges = (
        pltpu.make_async_copy(x_buf.at[pl.ds(0, rim)], low_hbm, edge_sem.at[0]),
        pltpu.make_async_copy(x_buf.at[pl.ds(points - rim, rim)], high_hbm, edge_sem.at[1]),
    )

    def rows_of(tile):
        return sum(tiles[:tile]), tiles[tile]

    def get_x(k, side):
        place = pl.ds(k * depth, depth)
        there = pl.ds(first + side * (cols // 2), width)
        return pltpu.make_async_copy(
            x_hbm.at[place, there], x_buf.at[place, pl.ds(side * width, width)], x_sem.at[k, side]
        )

    def get_s(tile):
        place = pl.ds(*rows_of(tile))
        return pltpu.make_async_copy(s_hbm.at[:, place], s_buf.at[:, place], s_sem.at[tile])

    def put(tile):
        place = pl.ds(*rows_of(tile))
        return pltpu.make_async_copy(held.at[place], out_hbm.at[place], out_sem.at[tile])

    def finish(tile, total):
        start, rows = rows_of(tile)
        place = lax.broadcasted_iota(jnp.int32, (RANK, 2 * width), 0)
        for group in range(rows // RANK):
            keep = place < rank_ref[start // RANK + group]
            part = total[group * RANK : (group + 1) * RANK]
            held[start + group * RANK : start + (group + 1) * RANK] = jnp.where(keep, part, 0.0).astype(jnp.bfloat16)
        put(tile).start()

    for k in range(min(parts, 2)):
        get_x(k, 0).start()
        get_x(k, 1).start()
        if k == 0:
            get_s(0).start()
    total = jnp.zeros((tiles[0], 2 * width), jnp.float32)
    for k in range(parts):
        get_x(k, 0).wait()
        get_x(k, 1).wait()
        own = slice(k * depth, (k + 1) * depth)
        turned = slice(points + k * depth, points + (k + 1) * depth)
        x = x_buf[own]
        if 2 * k * depth >= points:
            live = lax.broadcasted_iota(jnp.int32, x.shape, 0) + k * depth < count_ref[0]
            x = jnp.where(live, x.astype(jnp.float32), 0.0).astype(jnp.bfloat16)
            x_buf[own] = x
        x_buf[turned, :width] = -x[:, width:]
        x_buf[turned, width:] = x[:, :width]
        if k == 0:
            get_s(0).wait()
        if k + 2 < parts:
            get_x(k + 2, 0).start()
            get_x(k + 2, 1).start()
        if k == parts - 2:
            get_s(1).start()
        total += dot(s_buf[0, : tiles[0], own], x_buf[own]) + dot(s_buf[1, : tiles[0], own], x_buf[turned])
    finish(0, total)
    for edge in edges:
        edge.start()
    for tile in range(1, len(tiles)):
        start, rows = rows_of(tile)
        get_s(tile).wait()
        if tile + 1 < len(tiles):
            get_s(tile + 1).start()
        own = slice(start, start + rows)
        finish(tile, dot(jnp.concatenate([s_buf[0, own], s_buf[1, own]], axis=1), x_buf[...]))
    for edge in edges:
        edge.wait()
    for tile in range(len(tiles)):
        put(tile).wait()


def coefficients(count, rank, field, factor, depth=512, tiles=(256, 512, 1024, 256)):
    points, cols = field.shape
    total = factor.shape[1]
    width = cols // 2
    edge = jax.ShapeDtypeStruct((HALO_BLK * NEAR_B, cols), jnp.bfloat16)
    return pl.pallas_call(
        functools.partial(coeffs_kernel, tiles, depth),
        out_shape=[jax.ShapeDtypeStruct((total, cols), jnp.bfloat16), edge, edge],
        in_specs=[pl.BlockSpec(memory_space=pltpu.SMEM)] * 2 + [pl.BlockSpec(memory_space=pl.ANY)] * 2,
        out_specs=[pl.BlockSpec(memory_space=pl.ANY)] * 3,
        scratch_shapes=[
            pltpu.VMEM((2 * points, 2 * width), jnp.bfloat16),
            pltpu.VMEM((2, total, points), jnp.bfloat16),
            pltpu.VMEM((total, 2 * width), jnp.bfloat16),
            pltpu.SemaphoreType.DMA((points // depth, 2)),
            pltpu.SemaphoreType.DMA((len(tiles),)),
            pltpu.SemaphoreType.DMA((len(tiles),)),
            pltpu.SemaphoreType.DMA((2,)),
        ],
        compiler_params=params(60),
        cost_estimate=cost(8 * total * points * width, 4 * total * points + 4 * (points + total) * width),
        name="coeffs",
    )(count, rank, field, factor)


def near_kernel(index_ref, count_ref, low_ref, x_ref, high_ref, n_ref, out_ref, window):
    block = pl.program_id(0)
    points, cols = x_ref.shape
    half = cols // 2
    rim = HALO_BLK

    @pl.when(block == 0)
    def _():
        window[:rim] = low_ref[...].reshape(rim, NEAR_B, cols)
        window[rim + points // NEAR_B :] = high_ref[...].reshape(rim, NEAR_B, cols)
        for b in range(points // NEAR_B):
            live = lax.broadcasted_iota(jnp.int32, (NEAR_B, cols), 0) + b * NEAR_B < count_ref[0]
            part = x_ref[b * NEAR_B : (b + 1) * NEAR_B].astype(jnp.float32)
            window[rim + b] = jnp.where(live, part, 0.0).astype(jnp.bfloat16)

    p = jnp.zeros((NEAR_B, cols), jnp.float32)
    q = jnp.zeros((NEAR_B, cols), jnp.float32)
    for k in range(NB):
        x = window[index_ref[block * NB + k]]
        p += dot(n_ref[0, k], x)
        q += dot(n_ref[1, k], x)
    out_ref[:, :half] = p[:, :half] - q[:, half:]
    out_ref[:, half:] = p[:, half:] + q[:, :half]


def near_field(index, count, low, field, high, blocks):
    points, cols = field.shape
    rim = HALO_BLK * NEAR_B
    return pl.pallas_call(
        near_kernel,
        out_shape=jax.ShapeDtypeStruct((points, cols), jnp.float32),
        grid_spec=pltpu.PrefetchScalarGridSpec(
            num_scalar_prefetch=2,
            grid=(points // NEAR_B,),
            in_specs=[
                pl.BlockSpec((rim, cols), lambda i, *_: (0, 0)),
                pl.BlockSpec((points, cols), lambda i, *_: (0, 0)),
                pl.BlockSpec((rim, cols), lambda i, *_: (0, 0)),
                pl.BlockSpec((2, NB, NEAR_B, NEAR_B), lambda i, *_: (0, 0, i, 0)),
            ],
            out_specs=pl.BlockSpec((NEAR_B, cols), lambda i, *_: (i, 0)),
            scratch_shapes=[pltpu.VMEM((points // NEAR_B + 2 * HALO_BLK, NEAR_B, cols), jnp.bfloat16)],
        ),
        compiler_params=params(24),
        cost_estimate=cost(60_000_000_000, 6 * points * cols + 4 * points * NB * NEAR_B),
        name="near",
    )(index, count, low, field, high, blocks)


def far_kernel(
    tiles, part, count_ref, c_hbm, t_hbm, n_hbm, out_hbm, c_buf, t_buf, n_buf, held, c_sem, f_sem, t_sem, n_sem, out_sem
):
    depth, cols = c_hbm.shape
    half = cols // 2
    parts = depth // part

    def rows_of(tile):
        return sum(tiles[:tile]), tiles[tile]

    def get_c(k):
        place = pl.ds(k * part, part)
        return pltpu.make_async_copy(c_hbm.at[place], c_buf.at[place], c_sem.at[k])

    def get_first(k):
        rows, place = pl.ds(0, tiles[0]), pl.ds(k * part, part)
        return pltpu.make_async_copy(t_hbm.at[:, rows, place], t_buf.at[:, rows, place], f_sem.at[k])

    def get_t(tile):
        place = pl.ds(*rows_of(tile))
        return pltpu.make_async_copy(t_hbm.at[:, place], t_buf.at[:, place], t_sem.at[tile])

    def get_n(tile):
        place = pl.ds(*rows_of(tile))
        return pltpu.make_async_copy(n_hbm.at[place], n_buf.at[place], n_sem.at[tile])

    def put(tile):
        place = pl.ds(*rows_of(tile))
        return pltpu.make_async_copy(held.at[place], out_hbm.at[place], out_sem.at[tile])

    def finish(tile, pq):
        first, rows = rows_of(tile)
        get_n(tile).wait()
        own = slice(first, first + rows)
        live = lax.broadcasted_iota(jnp.int32, (rows, half), 0) + first < count_ref[0]
        real = pq[:rows, :half] - pq[rows:, half:] + n_buf[own, :half]
        imag = pq[:rows, half:] + pq[rows:, :half] + n_buf[own, half:]
        held[own, :half] = jnp.where(live, real, 0.0).astype(jnp.bfloat16)
        held[own, half:] = jnp.where(live, imag, 0.0).astype(jnp.bfloat16)
        put(tile).start()

    for k in range(parts):
        get_c(k).start()
        get_first(k).start()
    get_n(0).start()
    for tile in range(1, len(tiles)):
        get_t(tile).start()
        get_n(tile).start()
    pq = jnp.zeros((2 * tiles[0], cols), jnp.float32)
    for k in range(parts):
        get_c(k).wait()
        get_first(k).wait()
        own = slice(k * part, (k + 1) * part)
        pq += dot(t_buf[:, : tiles[0], own].reshape(2 * tiles[0], part), c_buf[own])
    finish(0, pq)
    for tile in range(1, len(tiles)):
        first, rows = rows_of(tile)
        get_t(tile).wait()
        finish(tile, dot(t_buf[:, first : first + rows].reshape(2 * rows, depth), c_buf[...]))
    for tile in range(len(tiles)):
        put(tile).wait()


def far_field(count, arrived, factor, near, part=512, tiles=(256, 512, 256)):
    points, cols = near.shape
    depth = arrived.shape[0]
    return pl.pallas_call(
        functools.partial(far_kernel, tiles, part),
        out_shape=jax.ShapeDtypeStruct((points, cols), jnp.bfloat16),
        in_specs=[pl.BlockSpec(memory_space=pltpu.SMEM)] + [pl.BlockSpec(memory_space=pl.ANY)] * 3,
        out_specs=pl.BlockSpec(memory_space=pl.ANY),
        scratch_shapes=[
            pltpu.VMEM((depth, cols), jnp.bfloat16),
            pltpu.VMEM((2, points, depth), jnp.bfloat16),
            pltpu.VMEM((points, cols), jnp.float32),
            pltpu.VMEM((points, cols), jnp.bfloat16),
            pltpu.SemaphoreType.DMA((depth // part,)),
            pltpu.SemaphoreType.DMA((depth // part,)),
            pltpu.SemaphoreType.DMA((len(tiles),)),
            pltpu.SemaphoreType.DMA((len(tiles),)),
            pltpu.SemaphoreType.DMA((len(tiles),)),
        ],
        compiler_params=params(60),
        cost_estimate=cost(4 * points * depth * cols, 4 * points * depth + 2 * depth * cols + 6 * points * cols),
        name="far",
    )(count, arrived, factor, near)


def halo(first, last):
    devices = lax.axis_size("cross")
    forward = [(i, i + 1) for i in range(devices - 1)]
    backward = [(target, source) for source, target in forward]
    return lax.ppermute(last, "cross", forward), lax.ppermute(first, "cross", backward)


def shards(surface_field, point_count, far_rank, source_factor, target_factor, near_blocks, near_index):
    boxes = far_rank.shape[1]
    cols = surface_field.shape[1]
    coeffs, first, last = coefficients(point_count, far_rank.reshape(boxes), surface_field, source_factor)
    low, high = halo(first, last)
    arrived = lax.all_to_all(coeffs.reshape(boxes, RANK, cols), AXES, split_axis=0, concat_axis=0, tiled=True)
    near = near_field(
        near_index.reshape(-1), point_count, low, surface_field, high, jnp.transpose(near_blocks, (0, 2, 1, 3))
    )
    return far_field(point_count, arrived.reshape(boxes * RANK, cols), target_factor, near)


def solution(mesh):
    return jax.shard_map(
        shards,
        mesh=mesh,
        in_specs=(
            P(AXES, None),
            P(AXES),
            P(AXES, None),
            P(None, None, AXES),
            P(None, AXES, None),
            P(None, AXES, None, None),
            P(AXES, None),
        ),
        out_specs=P(AXES, None),
        check_vma=False,
    )
```

```python
import functools

import jax
import jax.numpy as jnp
from jax import lax
from jax.experimental import pallas as pl
from jax.experimental.pallas import tpu as pltpu
from jax.sharding import PartitionSpec as P

RANK = 16
NEAR_B = 128
NB = 3
HALO_BLK = 2
AXES = ("range", "cross")
MIB = 1024 * 1024


def params(mib):
    return pltpu.CompilerParams(vmem_limit_bytes=mib * MIB)


def cost(flops, bytes_accessed):
    return pl.CostEstimate(flops=flops, bytes_accessed=bytes_accessed, transcendentals=0)


def dot(a, b):
    return jnp.dot(a, b, preferred_element_type=jnp.float32)


def coeffs_kernel(
    tiles, depth, count_ref, rank_ref, x_hbm, s_hbm, out_hbm, low_hbm, high_hbm,
    x_buf, s_buf, held, x_sem, s_sem, out_sem, edge_sem
):
    points, cols = x_hbm.shape
    width = cols // 2
    parts = points // depth
    rim = low_hbm.shape[0]
    first = 0
    edges = (
        pltpu.make_async_copy(x_buf.at[pl.ds(0, rim)], low_hbm, edge_sem.at[0]),
        pltpu.make_async_copy(x_buf.at[pl.ds(points - rim, rim)], high_hbm, edge_sem.at[1]),
    )

    def rows_of(tile):
        return sum(tiles[:tile]), tiles[tile]

    def get_x(k, side):
        place = pl.ds(k * depth, depth)
        there = pl.ds(first + side * (cols // 2), width)
        return pltpu.make_async_copy(
            x_hbm.at[place, there], x_buf.at[place, pl.ds(side * width, width)], x_sem.at[k, side]
        )

    def get_s(tile):
        place = pl.ds(*rows_of(tile))
        return pltpu.make_async_copy(s_hbm.at[:, place], s_buf.at[:, place], s_sem.at[tile])

    def put(tile):
        place = pl.ds(*rows_of(tile))
        return pltpu.make_async_copy(held.at[place], out_hbm.at[place], out_sem.at[tile])

    def finish(tile, total):
        start, rows = rows_of(tile)
        place = lax.broadcasted_iota(jnp.int32, (RANK, 2 * width), 0)
        for group in range(rows // RANK):
            keep = place < rank_ref[start // RANK + group]
            part = total[group * RANK : (group + 1) * RANK]
            held[start + group * RANK : start + (group + 1) * RANK] = jnp.where(keep, part, 0.0).astype(jnp.bfloat16)
        put(tile).start()

    for k in range(min(parts, 2)):
        get_x(k, 0).start()
        get_x(k, 1).start()
        if k == 0:
            get_s(0).start()
    total = jnp.zeros((tiles[0], 2 * width), jnp.float32)
    for k in range(parts):
        get_x(k, 0).wait()
        get_x(k, 1).wait()
        own = slice(k * depth, (k + 1) * depth)
        turned = slice(points + k * depth, points + (k + 1) * depth)
        x = x_buf[own]
        if 2 * k * depth >= points:
            live = lax.broadcasted_iota(jnp.int32, x.shape, 0) + k * depth < count_ref[0]
            x = jnp.where(live, x.astype(jnp.float32), 0.0).astype(jnp.bfloat16)
            x_buf[own] = x
        x_buf[turned, :width] = -x[:, width:]
        x_buf[turned, width:] = x[:, :width]
        if k == 0:
            get_s(0).wait()
        if k + 2 < parts:
            get_x(k + 2, 0).start()
            get_x(k + 2, 1).start()
        if k == parts - 2:
            get_s(1).start()
        total += dot(s_buf[0, : tiles[0], own], x_buf[own]) + dot(s_buf[1, : tiles[0], own], x_buf[turned])
    finish(0, total)
    for edge in edges:
        edge.start()
    for tile in range(1, len(tiles)):
        start, rows = rows_of(tile)
        get_s(tile).wait()
        if tile + 1 < len(tiles):
            get_s(tile + 1).start()
        own = slice(start, start + rows)
        finish(tile, dot(jnp.concatenate([s_buf[0, own], s_buf[1, own]], axis=1), x_buf[...]))
    for edge in edges:
        edge.wait()
    for tile in range(len(tiles)):
        put(tile).wait()


def coefficients(count, rank, field, factor, depth=512, tiles=(256, 512, 1024, 256)):
    points, cols = field.shape
    total = factor.shape[1]
    width = cols // 2
    edge = jax.ShapeDtypeStruct((HALO_BLK * NEAR_B, cols), jnp.bfloat16)
    return pl.pallas_call(
        functools.partial(coeffs_kernel, tiles, depth),
        out_shape=[jax.ShapeDtypeStruct((total, cols), jnp.bfloat16), edge, edge],
        in_specs=[pl.BlockSpec(memory_space=pltpu.SMEM)] * 2 + [pl.BlockSpec(memory_space=pl.ANY)] * 2,
        out_specs=[pl.BlockSpec(memory_space=pl.ANY)] * 3,
        scratch_shapes=[
            pltpu.VMEM((2 * points, 2 * width), jnp.bfloat16),
            pltpu.VMEM((2, total, points), jnp.bfloat16),
            pltpu.VMEM((total, 2 * width), jnp.bfloat16),
            pltpu.SemaphoreType.DMA((points // depth, 2)),
            pltpu.SemaphoreType.DMA((len(tiles),)),
            pltpu.SemaphoreType.DMA((len(tiles),)),
            pltpu.SemaphoreType.DMA((2,)),
        ],
        compiler_params=params(60),
        cost_estimate=cost(8 * total * points * width, 4 * total * points + 4 * (points + total) * width),
        name="coeffs",
    )(count, rank, field, factor)


def near_kernel(index_ref, count_ref, low_ref, x_ref, high_ref, n_ref, out_ref, window):
    block = pl.program_id(0)
    points, cols = x_ref.shape
    half = cols // 2
    rim = HALO_BLK

    @pl.when(block == 0)
    def _():
        window[:rim] = low_ref[...].reshape(rim, NEAR_B, cols)
        window[rim + points // NEAR_B :] = high_ref[...].reshape(rim, NEAR_B, cols)
        for b in range(points // NEAR_B):
            live = lax.broadcasted_iota(jnp.int32, (NEAR_B, cols), 0) + b * NEAR_B < count_ref[0]
            part = x_ref[b * NEAR_B : (b + 1) * NEAR_B].astype(jnp.float32)
            window[rim + b] = jnp.where(live, part, 0.0).astype(jnp.bfloat16)

    p = jnp.zeros((NEAR_B, cols), jnp.float32)
    q = jnp.zeros((NEAR_B, cols), jnp.float32)
    for k in range(NB):
        x = window[index_ref[block * NB + k]]
        p += dot(n_ref[0, k], x)
        q += dot(n_ref[1, k], x)
    out_ref[:, :half] = (p[:, :half] - q[:, half:]).astype(out_ref.dtype)
    out_ref[:, half:] = (p[:, half:] + q[:, :half]).astype(out_ref.dtype)


def near_field(index, count, low, field, high, blocks):
    points, cols = field.shape
    rim = HALO_BLK * NEAR_B
    return pl.pallas_call(
        near_kernel,
        out_shape=jax.ShapeDtypeStruct((points, cols), jnp.bfloat16),
        grid_spec=pltpu.PrefetchScalarGridSpec(
            num_scalar_prefetch=2,
            grid=(points // NEAR_B,),
            in_specs=[
                pl.BlockSpec((rim, cols), lambda i, *_: (0, 0)),
                pl.BlockSpec((points, cols), lambda i, *_: (0, 0)),
                pl.BlockSpec((rim, cols), lambda i, *_: (0, 0)),
                pl.BlockSpec((2, NB, NEAR_B, NEAR_B), lambda i, *_: (0, 0, i, 0)),
            ],
            out_specs=pl.BlockSpec((NEAR_B, cols), lambda i, *_: (i, 0)),
            scratch_shapes=[pltpu.VMEM((points // NEAR_B + 2 * HALO_BLK, NEAR_B, cols), jnp.bfloat16)],
        ),
        compiler_params=params(24),
        cost_estimate=cost(60_000_000_000, 6 * points * cols + 4 * points * NB * NEAR_B),
        name="near",
    )(index, count, low, field, high, blocks)


def far_kernel(
    tiles, part, count_ref, c_hbm, t_hbm, n_hbm, out_hbm, c_buf, t_buf, n_buf, held, c_sem, f_sem, t_sem, n_sem, out_sem
):
    depth, cols = c_hbm.shape
    half = cols // 2
    parts = depth // part

    def rows_of(tile):
        return sum(tiles[:tile]), tiles[tile]

    def get_c(k):
        place = pl.ds(k * part, part)
        return pltpu.make_async_copy(c_hbm.at[place], c_buf.at[place], c_sem.at[k])

    def get_first(k):
        rows, place = pl.ds(0, tiles[0]), pl.ds(k * part, part)
        return pltpu.make_async_copy(t_hbm.at[:, rows, place], t_buf.at[:, rows, place], f_sem.at[k])

    def get_t(tile):
        place = pl.ds(*rows_of(tile))
        return pltpu.make_async_copy(t_hbm.at[:, place], t_buf.at[:, place], t_sem.at[tile])

    def get_n(tile):
        place = pl.ds(*rows_of(tile))
        return pltpu.make_async_copy(n_hbm.at[place], n_buf.at[place], n_sem.at[tile])

    def put(tile):
        place = pl.ds(*rows_of(tile))
        return pltpu.make_async_copy(held.at[place], out_hbm.at[place], out_sem.at[tile])

    def finish(tile, pq):
        first, rows = rows_of(tile)
        get_n(tile).wait()
        own = slice(first, first + rows)
        live = lax.broadcasted_iota(jnp.int32, (rows, half), 0) + first < count_ref[0]
        real = pq[:rows, :half] - pq[rows:, half:] + n_buf[own, :half].astype(jnp.float32)
        imag = pq[:rows, half:] + pq[rows:, :half] + n_buf[own, half:].astype(jnp.float32)
        held[own, :half] = jnp.where(live, real, 0.0).astype(jnp.bfloat16)
        held[own, half:] = jnp.where(live, imag, 0.0).astype(jnp.bfloat16)
        put(tile).start()

    for k in range(parts):
        get_c(k).start()
        get_first(k).start()
    get_n(0).start()
    for tile in range(1, len(tiles)):
        get_t(tile).start()
        get_n(tile).start()
    pq = jnp.zeros((2 * tiles[0], cols), jnp.float32)
    for k in range(parts):
        get_c(k).wait()
        get_first(k).wait()
        own = slice(k * part, (k + 1) * part)
        pq += dot(t_buf[:, : tiles[0], own].reshape(2 * tiles[0], part), c_buf[own])
    finish(0, pq)
    for tile in range(1, len(tiles)):
        first, rows = rows_of(tile)
        get_t(tile).wait()
        finish(tile, dot(t_buf[:, first : first + rows].reshape(2 * rows, depth), c_buf[...]))
    for tile in range(len(tiles)):
        put(tile).wait()


def far_field(count, arrived, factor, near, part=512, tiles=(256, 512, 256)):
    points, cols = near.shape
    depth = arrived.shape[0]
    return pl.pallas_call(
        functools.partial(far_kernel, tiles, part),
        out_shape=jax.ShapeDtypeStruct((points, cols), jnp.bfloat16),
        in_specs=[pl.BlockSpec(memory_space=pltpu.SMEM)] + [pl.BlockSpec(memory_space=pl.ANY)] * 3,
        out_specs=pl.BlockSpec(memory_space=pl.ANY),
        scratch_shapes=[
            pltpu.VMEM((depth, cols), jnp.bfloat16),
            pltpu.VMEM((2, points, depth), jnp.bfloat16),
            pltpu.VMEM((points, cols), jnp.bfloat16),
            pltpu.VMEM((points, cols), jnp.bfloat16),
            pltpu.SemaphoreType.DMA((depth // part,)),
            pltpu.SemaphoreType.DMA((depth // part,)),
            pltpu.SemaphoreType.DMA((len(tiles),)),
            pltpu.SemaphoreType.DMA((len(tiles),)),
            pltpu.SemaphoreType.DMA((len(tiles),)),
        ],
        compiler_params=params(60),
        cost_estimate=cost(4 * points * depth * cols, 4 * points * depth + 2 * depth * cols + 6 * points * cols),
        name="far",
    )(count, arrived, factor, near)


def halo(first, last):
    devices = lax.axis_size("cross")
    forward = [(i, i + 1) for i in range(devices - 1)]
    backward = [(target, source) for source, target in forward]
    return lax.ppermute(last, "cross", forward), lax.ppermute(first, "cross", backward)


def shards(surface_field, point_count, far_rank, source_factor, target_factor, near_blocks, near_index):
    boxes = far_rank.shape[1]
    cols = surface_field.shape[1]
    coeffs, first, last = coefficients(point_count, far_rank.reshape(boxes), surface_field, source_factor)
    low, high = halo(first, last)
    arrived = lax.all_to_all(coeffs.reshape(boxes, RANK, cols), AXES, split_axis=0, concat_axis=0, tiled=True)
    near = near_field(
        near_index.reshape(-1), point_count, low, surface_field, high, jnp.transpose(near_blocks, (0, 2, 1, 3))
    )
    return far_field(point_count, arrived.reshape(boxes * RANK, cols), target_factor, near)


def solution(mesh):
    return jax.shard_map(
        shards,
        mesh=mesh,
        in_specs=(
            P(AXES, None),
            P(AXES),
            P(AXES, None),
            P(None, None, AXES),
            P(None, AXES, None),
            P(None, AXES, None, None),
            P(AXES, None),
        ),
        out_specs=P(AXES, None),
        check_vma=False,
    )
```

```python
import functools

import jax
import jax.numpy as jnp
from jax import lax
from jax.experimental import pallas as pl
from jax.experimental.pallas import tpu as pltpu
from jax.sharding import PartitionSpec as P

RANK = 16
NEAR_B = 128
NB = 3
HALO_BLK = 2
AXES = ("range", "cross")
MIB = 1024 * 1024


def params(mib):
    return pltpu.CompilerParams(vmem_limit_bytes=mib * MIB)


def cost(flops, bytes_accessed):
    return pl.CostEstimate(flops=flops, bytes_accessed=bytes_accessed, transcendentals=0)


def dot(a, b):
    return jnp.dot(a, b, preferred_element_type=jnp.float32)


def coeffs_kernel(
    tiles, depth, count_ref, rank_ref, x_hbm, s_hbm, out_hbm, low_hbm, high_hbm,
    x_buf, s_buf, held, x_sem, s_sem, out_sem, edge_sem
):
    points, cols = x_hbm.shape
    width = cols // 2
    parts = points // depth
    rim = low_hbm.shape[0]
    first = 0
    odd = lax.rem(lax.axis_index("cross"), 2)
    inner, outer = (1 - odd) * (points - rim), odd * (points - rim)
    edges = (
        pltpu.make_async_copy(x_buf.at[pl.ds(pl.multiple_of(inner, rim), rim)], low_hbm, edge_sem.at[0]),
        pltpu.make_async_copy(x_buf.at[pl.ds(pl.multiple_of(outer, rim), rim)], high_hbm, edge_sem.at[1]),
    )

    def rows_of(tile):
        return sum(tiles[:tile]), tiles[tile]

    def get_x(k, side):
        place = pl.ds(k * depth, depth)
        there = pl.ds(first + side * (cols // 2), width)
        return pltpu.make_async_copy(
            x_hbm.at[place, there], x_buf.at[place, pl.ds(side * width, width)], x_sem.at[k, side]
        )

    def get_s(tile):
        place = pl.ds(*rows_of(tile))
        return pltpu.make_async_copy(s_hbm.at[:, place], s_buf.at[:, place], s_sem.at[tile])

    def put(tile):
        place = pl.ds(*rows_of(tile))
        return pltpu.make_async_copy(held.at[place], out_hbm.at[place], out_sem.at[tile])

    def finish(tile, total):
        start, rows = rows_of(tile)
        place = lax.broadcasted_iota(jnp.int32, (RANK, 2 * width), 0)
        for group in range(rows // RANK):
            keep = place < rank_ref[start // RANK + group]
            part = total[group * RANK : (group + 1) * RANK]
            held[start + group * RANK : start + (group + 1) * RANK] = jnp.where(keep, part, 0.0).astype(jnp.bfloat16)
        put(tile).start()

    for k in range(min(parts, 2)):
        get_x(k, 0).start()
        get_x(k, 1).start()
        if k == 0:
            get_s(0).start()
    total = jnp.zeros((tiles[0], 2 * width), jnp.float32)
    for k in range(parts):
        get_x(k, 0).wait()
        get_x(k, 1).wait()
        own = slice(k * depth, (k + 1) * depth)
        turned = slice(points + k * depth, points + (k + 1) * depth)
        x = x_buf[own]
        if 2 * k * depth >= points:
            live = lax.broadcasted_iota(jnp.int32, x.shape, 0) + k * depth < count_ref[0]
            x = jnp.where(live, x.astype(jnp.float32), 0.0).astype(jnp.bfloat16)
            x_buf[own] = x
        x_buf[turned, :width] = -x[:, width:]
        x_buf[turned, width:] = x[:, :width]
        if k == 0:
            get_s(0).wait()
        if k + 2 < parts:
            get_x(k + 2, 0).start()
            get_x(k + 2, 1).start()
        if k == parts - 2:
            get_s(1).start()
        total += dot(s_buf[0, : tiles[0], own], x_buf[own]) + dot(s_buf[1, : tiles[0], own], x_buf[turned])
    finish(0, total)
    for edge in edges:
        edge.start()
    for tile in range(1, len(tiles)):
        start, rows = rows_of(tile)
        get_s(tile).wait()
        if tile + 1 < len(tiles):
            get_s(tile + 1).start()
        own = slice(start, start + rows)
        finish(tile, dot(jnp.concatenate([s_buf[0, own], s_buf[1, own]], axis=1), x_buf[...]))
    for edge in edges:
        edge.wait()
    for tile in range(len(tiles)):
        put(tile).wait()


def coefficients(count, rank, field, factor, depth=512, tiles=(256, 512, 1024, 256)):
    points, cols = field.shape
    total = factor.shape[1]
    width = cols // 2
    edge = jax.ShapeDtypeStruct((HALO_BLK * NEAR_B, cols), jnp.bfloat16)
    return pl.pallas_call(
        functools.partial(coeffs_kernel, tiles, depth),
        out_shape=[jax.ShapeDtypeStruct((total, cols), jnp.bfloat16), edge, edge],
        in_specs=[pl.BlockSpec(memory_space=pltpu.SMEM)] * 2 + [pl.BlockSpec(memory_space=pl.ANY)] * 2,
        out_specs=[pl.BlockSpec(memory_space=pl.ANY)] * 3,
        scratch_shapes=[
            pltpu.VMEM((2 * points, 2 * width), jnp.bfloat16),
            pltpu.VMEM((2, total, points), jnp.bfloat16),
            pltpu.VMEM((total, 2 * width), jnp.bfloat16),
            pltpu.SemaphoreType.DMA((points // depth, 2)),
            pltpu.SemaphoreType.DMA((len(tiles),)),
            pltpu.SemaphoreType.DMA((len(tiles),)),
            pltpu.SemaphoreType.DMA((2,)),
        ],
        compiler_params=params(60),
        cost_estimate=cost(8 * total * points * width, 4 * total * points + 4 * (points + total) * width),
        name="coeffs",
    )(count, rank, field, factor)


def near_kernel(index_ref, count_ref, low_ref, x_ref, high_ref, n_ref, out_ref, window):
    block = pl.program_id(0)
    points, cols = x_ref.shape
    half = cols // 2
    rim = HALO_BLK

    @pl.when(block == 0)
    def _():
        window[:rim] = low_ref[...].reshape(rim, NEAR_B, cols)
        window[rim + points // NEAR_B :] = high_ref[...].reshape(rim, NEAR_B, cols)
        for b in range(points // NEAR_B):
            live = lax.broadcasted_iota(jnp.int32, (NEAR_B, cols), 0) + b * NEAR_B < count_ref[0]
            part = x_ref[b * NEAR_B : (b + 1) * NEAR_B].astype(jnp.float32)
            window[rim + b] = jnp.where(live, part, 0.0).astype(jnp.bfloat16)

    p = jnp.zeros((NEAR_B, cols), jnp.float32)
    q = jnp.zeros((NEAR_B, cols), jnp.float32)
    for k in range(NB):
        x = window[index_ref[block * NB + k]]
        p += dot(n_ref[0, k], x)
        q += dot(n_ref[1, k], x)
    out_ref[:, :half] = p[:, :half] - q[:, half:]
    out_ref[:, half:] = p[:, half:] + q[:, :half]


def near_field(index, count, low, field, high, blocks):
    points, cols = field.shape
    rim = HALO_BLK * NEAR_B
    return pl.pallas_call(
        near_kernel,
        out_shape=jax.ShapeDtypeStruct((points, cols), jnp.float32),
        grid_spec=pltpu.PrefetchScalarGridSpec(
            num_scalar_prefetch=2,
            grid=(points // NEAR_B,),
            in_specs=[
                pl.BlockSpec((rim, cols), lambda i, *_: (0, 0)),
                pl.BlockSpec((points, cols), lambda i, *_: (0, 0)),
                pl.BlockSpec((rim, cols), lambda i, *_: (0, 0)),
                pl.BlockSpec((2, NB, NEAR_B, NEAR_B), lambda i, *_: (0, 0, i, 0)),
            ],
            out_specs=pl.BlockSpec((NEAR_B, cols), lambda i, *_: (i, 0)),
            scratch_shapes=[pltpu.VMEM((points // NEAR_B + 2 * HALO_BLK, NEAR_B, cols), jnp.bfloat16)],
        ),
        compiler_params=params(24),
        cost_estimate=cost(60_000_000_000, 6 * points * cols + 4 * points * NB * NEAR_B),
        name="near",
    )(index, count, low, field, high, blocks)


def far_kernel(
    tiles, part, count_ref, c_hbm, t_hbm, n_hbm, out_hbm, c_buf, t_buf, n_buf, held, c_sem, f_sem, t_sem, n_sem, out_sem
):
    depth, cols = c_hbm.shape
    half = cols // 2
    parts = depth // part

    def rows_of(tile):
        return sum(tiles[:tile]), tiles[tile]

    def get_c(k):
        place = pl.ds(k * part, part)
        return pltpu.make_async_copy(c_hbm.at[place], c_buf.at[place], c_sem.at[k])

    def get_first(k):
        rows, place = pl.ds(0, tiles[0]), pl.ds(k * part, part)
        return pltpu.make_async_copy(t_hbm.at[:, rows, place], t_buf.at[:, rows, place], f_sem.at[k])

    def get_t(tile):
        place = pl.ds(*rows_of(tile))
        return pltpu.make_async_copy(t_hbm.at[:, place], t_buf.at[:, place], t_sem.at[tile])

    def get_n(tile):
        place = pl.ds(*rows_of(tile))
        return pltpu.make_async_copy(n_hbm.at[place], n_buf.at[place], n_sem.at[tile])

    def put(tile):
        place = pl.ds(*rows_of(tile))
        return pltpu.make_async_copy(held.at[place], out_hbm.at[place], out_sem.at[tile])

    def finish(tile, pq):
        first, rows = rows_of(tile)
        get_n(tile).wait()
        own = slice(first, first + rows)
        live = lax.broadcasted_iota(jnp.int32, (rows, half), 0) + first < count_ref[0]
        real = pq[:rows, :half] - pq[rows:, half:] + n_buf[own, :half]
        imag = pq[:rows, half:] + pq[rows:, :half] + n_buf[own, half:]
        held[own, :half] = jnp.where(live, real, 0.0).astype(jnp.bfloat16)
        held[own, half:] = jnp.where(live, imag, 0.0).astype(jnp.bfloat16)
        put(tile).start()

    for k in range(parts):
        get_c(k).start()
        get_first(k).start()
    get_n(0).start()
    for tile in range(1, len(tiles)):
        get_t(tile).start()
        get_n(tile).start()
    pq = jnp.zeros((2 * tiles[0], cols), jnp.float32)
    for k in range(parts):
        get_c(k).wait()
        get_first(k).wait()
        own = slice(k * part, (k + 1) * part)
        pq += dot(t_buf[:, : tiles[0], own].reshape(2 * tiles[0], part), c_buf[own])
    finish(0, pq)
    for tile in range(1, len(tiles)):
        first, rows = rows_of(tile)
        get_t(tile).wait()
        finish(tile, dot(t_buf[:, first : first + rows].reshape(2 * rows, depth), c_buf[...]))
    for tile in range(len(tiles)):
        put(tile).wait()


def far_field(count, arrived, factor, near, part=512, tiles=(256, 512, 256)):
    points, cols = near.shape
    depth = arrived.shape[0]
    return pl.pallas_call(
        functools.partial(far_kernel, tiles, part),
        out_shape=jax.ShapeDtypeStruct((points, cols), jnp.bfloat16),
        in_specs=[pl.BlockSpec(memory_space=pltpu.SMEM)] + [pl.BlockSpec(memory_space=pl.ANY)] * 3,
        out_specs=pl.BlockSpec(memory_space=pl.ANY),
        scratch_shapes=[
            pltpu.VMEM((depth, cols), jnp.bfloat16),
            pltpu.VMEM((2, points, depth), jnp.bfloat16),
            pltpu.VMEM((points, cols), jnp.float32),
            pltpu.VMEM((points, cols), jnp.bfloat16),
            pltpu.SemaphoreType.DMA((depth // part,)),
            pltpu.SemaphoreType.DMA((depth // part,)),
            pltpu.SemaphoreType.DMA((len(tiles),)),
            pltpu.SemaphoreType.DMA((len(tiles),)),
            pltpu.SemaphoreType.DMA((len(tiles),)),
        ],
        compiler_params=params(60),
        cost_estimate=cost(4 * points * depth * cols, 4 * points * depth + 2 * depth * cols + 6 * points * cols),
        name="far",
    )(count, arrived, factor, near)


def halo(inner, outer):
    devices = lax.axis_size("cross")
    pairs = [[(i, i + 1) for i in range(start, devices - 1, 2)] for start in (0, 1)]
    swaps = [one + [(b, a) for a, b in one] for one in pairs]
    inner, outer = lax.ppermute(inner, "cross", swaps[0]), lax.ppermute(outer, "cross", swaps[1])
    even = lax.rem(lax.axis_index("cross"), 2) == 0
    return jnp.where(even, outer, inner), jnp.where(even, inner, outer)


def shards(surface_field, point_count, far_rank, source_factor, target_factor, near_blocks, near_index):
    boxes = far_rank.shape[1]
    cols = surface_field.shape[1]
    coeffs, first, last = coefficients(point_count, far_rank.reshape(boxes), surface_field, source_factor)
    low, high = halo(first, last)
    arrived = lax.all_to_all(coeffs.reshape(boxes, RANK, cols), AXES, split_axis=0, concat_axis=0, tiled=True)
    near = near_field(
        near_index.reshape(-1), point_count, low, surface_field, high, jnp.transpose(near_blocks, (0, 2, 1, 3))
    )
    return far_field(point_count, arrived.reshape(boxes * RANK, cols), target_factor, near)


def solution(mesh):
    return jax.shard_map(
        shards,
        mesh=mesh,
        in_specs=(
            P(AXES, None),
            P(AXES),
            P(AXES, None),
            P(None, None, AXES),
            P(None, AXES, None),
            P(None, AXES, None, None),
            P(AXES, None),
        ),
        out_specs=P(AXES, None),
        check_vma=False,
    )
```
